32 devices in a mesh: ctx: 8 (over y, x, core), fsdp: 4 (over z).
Axes of the slice: x: 2, y: 2, z: 4, core: 2. Of those that a mesh axis runs over, the one named last changes fastest.
Arguments:
- tokens_in: bfloat16 [4096, 5376], P('ctx'), may hold values from -6 to 6
- query: bfloat16 [4096, 1024], P('ctx', 'fsdp'), may hold values from -6 to 6
- key: bfloat16 [4096, 512], P('ctx', 'fsdp'), may hold values from -6 to 6
- value: bfloat16 [4096, 512], P('ctx', 'fsdp'), may hold values from -6 to 6
- d_out: bfloat16 [4096, 1024], P('ctx', 'fsdp'), may hold values from -6 to 6
- seg_ids: int32 [4096], P('ctx'), may hold values from 0 to 3, as said below
Outputs:
- d_query: bfloat16 [4096, 1024], P('ctx', 'fsdp')
- d_key: bfloat16 [4096, 512], P('ctx', 'fsdp')
- d_value: bfloat16 [4096, 512], P('ctx', 'fsdp')
- dw_key: float32 [5376, 512], P('ctx', 'fsdp')
- dw_value: float32 [5376, 512], P('ctx', 'fsdp')
The draws below stay inside these ranges and needn't reach their ends.
Inputs may be any that keep to these rules, and one draw needn't show every extreme that they name: `seg_ids`: never falls along the sequence, starts at 0 and rises by at most one from a token to the next; every segment number is used.
All inputs are finite; a program needn't handle non-finite values.
Results may differ from the reference program's by a relative error of at most 0.014.
Values may be sent and summed in bfloat16 or wider, within the bound.
A program may use at most 64 MiB of HBM per device.

```python
import jax
import jax.numpy as jnp
from jax import lax

D = 5376
HD = 128
GROUP = 2
WINDOW = 1024
TOK_DEV = 512
SEQ = 4096
HK = 4
HQ = 8
N_CTX = 8


def draw_query(key, part):
    own = jax.random.fold_in(key, 11)
    values = jax.random.normal(own, (SEQ, HQ * HD), jnp.float32)
    return jnp.clip(values, -6.0, 6.0).astype(jnp.bfloat16)


def draw_key(key, part):
    own = jax.random.fold_in(key, 17)
    values = jax.random.normal(own, (SEQ, HK * HD), jnp.float32)
    return jnp.clip(values, -6.0, 6.0).astype(jnp.bfloat16)


def draw_seg_ids(key, part):
    own = jax.random.fold_in(key, 23)
    order = jax.random.permutation(own, SEQ - 1).astype(jnp.int32)
    cuts = order[:N_CTX // 2 - 1] + 1
    positions = jnp.arange(SEQ, dtype=jnp.int32)
    return jnp.sum((positions[:, None] >= cuts[None, :]).astype(jnp.int32), 1).astype(jnp.int32)


def raised(array, own_key, source, target, parts, factor):
    def block_of(dim):
        return (jnp.arange(array.shape[dim]) // (array.shape[dim] // parts)).reshape((-1,) + (1,) * (array.ndim - 1 - dim))

    first = jax.random.permutation(own_key, parts)[block_of(target)]
    far = (block_of(target) + parts // 2) % parts
    return jnp.where((block_of(source) == first) | (block_of(source) == far), factor * array, array)


def level_of(stream_key, shape, cuts, smallest, largest):
    factor_of = 1.0
    for dim, shards_of in cuts:
        draws = jax.random.uniform(jax.random.fold_in(jax.random.fold_in(stream_key, 6), dim), (shards_of,), jnp.float32, smallest / len(cuts), largest / len(cuts))
        factor_of = factor_of * jnp.repeat(jnp.exp(draws), shape[dim] // shards_of).reshape((-1,) + (1,) * (len(shape) - 1 - dim))
    return factor_of


def noise(stream_key, extent, deviation, most, shards=(), held_as=jnp.bfloat16):
    factor_of = level_of(stream_key, extent, shards, -0.22, 0.18) if shards else 1.0
    entries = jax.random.normal(stream_key, extent, jnp.float32) * deviation * factor_of
    return jnp.minimum(jnp.maximum(entries, -most), most).astype(held_as)


def gaussian_with(stream_key, shape, spread, limit, cuts, heavy, kind=jnp.bfloat16):
    entries = spread * jax.random.normal(stream_key, shape, jnp.float32)
    if cuts:
        entries = entries * level_of(stream_key, shape, cuts, -0.22, 0.18)
    return jnp.clip(raised(entries, jax.random.fold_in(stream_key, 3), *heavy), -limit, limit).astype(kind)


def setup_inputs(seed: int = 0) -> dict:
    keys = jax.random.split(jax.random.key(seed), 7)
    return {
        "tokens_in": gaussian_with(keys[0], (SEQ, D), 1.0, 6.0, ((0, 8),), (0, 1, 8, 2.0)),
        "query": draw_query(jax.random.fold_in(keys[6], 71), 0),
        "key": draw_key(jax.random.fold_in(keys[6], 71), 0),
        "value": noise(keys[3], (SEQ, HK * HD), 1.0, 6.0, ((0, 8), (1, 4))),
        "d_out": noise(keys[4], (SEQ, HQ * HD), 1.0, 6.0, ((0, 8), (1, 4))),
        "seg_ids": draw_seg_ids(jax.random.fold_in(keys[6], 71), 0),
    }


query_scale = 168.0 ** -0.5
masked_score = -1e30


def reference(tokens_in, query, key, value, d_out, seg_ids):
    hops = WINDOW // TOK_DEV
    span = (hops + 1) * TOK_DEV
    margin = hops * TOK_DEV
    q_heads = query.reshape(SEQ, HK, GROUP, HD)
    grad_heads = d_out.reshape(SEQ, HK, GROUP, HD)
    key_pad = jnp.concatenate([jnp.zeros((margin, HK * HD), key.dtype), key], 0).reshape(SEQ + margin, HK, HD)
    value_pad = jnp.concatenate([jnp.zeros((margin, HK * HD), value.dtype), value], 0).reshape(SEQ + margin, HK, HD)
    seg_pad = jnp.concatenate([jnp.full((margin,), -1, jnp.int32), seg_ids.astype(jnp.int32)], 0)

    def slab(accum, index):
        start = (index * TOK_DEV).astype(jnp.int32)
        q_slab = lax.dynamic_slice_in_dim(q_heads, start, TOK_DEV, 0).astype(jnp.float32)
        g_slab = lax.dynamic_slice_in_dim(grad_heads, start, TOK_DEV, 0).astype(jnp.float32)
        k_slab = lax.dynamic_slice_in_dim(key_pad, start, span, 0).astype(jnp.float32)
        v_slab = lax.dynamic_slice_in_dim(value_pad, start, span, 0).astype(jnp.float32)
        seg_q = lax.dynamic_slice_in_dim(seg_ids.astype(jnp.int32), start, TOK_DEV, 0)
        seg_k = lax.dynamic_slice_in_dim(seg_pad, start, span, 0)
        q_pos = start + jnp.arange(TOK_DEV, dtype=jnp.int32)
        k_pos = start - margin + jnp.arange(span, dtype=jnp.int32)
        allowed = (k_pos[None, :] <= q_pos[:, None]) & (q_pos[:, None] - k_pos[None, :] < WINDOW)
        allowed = allowed & (k_pos[None, :] >= 0) & (seg_q[:, None] == seg_k[None, :])
        scores = jnp.einsum("ihgd,jhd->hgij", q_slab, k_slab) * query_scale
        scores = jnp.where(allowed[None, None], scores, masked_score)
        top = jnp.max(scores, -1, keepdims=True)
        expo = jnp.exp(scores - top)
        probs = expo / jnp.sum(expo, -1, keepdims=True)
        probs_b = probs.astype(jnp.bfloat16).astype(jnp.float32)
        attended = jnp.einsum("hgij,jhd->ihgd", probs_b, v_slab)
        delta = jnp.transpose(jnp.sum(g_slab * attended, -1), (1, 2, 0))[..., None]
        dprob = jnp.einsum("ihgd,jhd->hgij", g_slab, v_slab)
        dscore = (probs * (dprob - delta)).astype(jnp.bfloat16).astype(jnp.float32)
        dq_slab = jnp.einsum("hgij,jhd->ihgd", dscore, k_slab) * query_scale
        dk_slab = jnp.einsum("hgij,ihgd->jhd", dscore, q_slab) * query_scale
        dv_slab = jnp.einsum("hgij,ihgd->jhd", probs_b, g_slab)
        contrib = jnp.stack([dk_slab, dv_slab], 2)
        zero = jnp.zeros((), jnp.int32)
        old = lax.dynamic_slice(accum, (start, zero, zero, zero), contrib.shape)
        accum = lax.dynamic_update_slice(accum, old + contrib, (start, zero, zero, zero))
        return accum, dq_slab.astype(jnp.bfloat16)

    accum0 = jnp.zeros((SEQ + margin, HK, 2, HD), jnp.float32)
    accum, dq_slabs = lax.scan(slab, accum0, jnp.arange(N_CTX, dtype=jnp.int32))
    d_query = dq_slabs.reshape(SEQ, HQ * HD)
    d_key = accum[margin:, :, 0, :].reshape(SEQ, HK * HD).astype(jnp.bfloat16)
    d_value = accum[margin:, :, 1, :].reshape(SEQ, HK * HD).astype(jnp.bfloat16)
    grads_both = jnp.concatenate([d_key, d_value], 1)

    def weight_slab(total, index):
        start = (index * TOK_DEV).astype(jnp.int32)
        rows_in = lax.dynamic_slice_in_dim(tokens_in, start, TOK_DEV, 0)
        rows_grad = lax.dynamic_slice_in_dim(grads_both, start, TOK_DEV, 0)
        partial_term = jnp.dot(rows_in.T, rows_grad, preferred_element_type=jnp.float32)
        rounded = lax.optimization_barrier(partial_term.astype(jnp.bfloat16)).astype(jnp.float32)
        return total + rounded, None

    total0 = jnp.zeros((D, 2 * HK * HD), jnp.float32)
    summed, unused = lax.scan(weight_slab, total0, jnp.arange(N_CTX, dtype=jnp.int32))
    dw_key = summed[:, :HK * HD]
    dw_value = summed[:, HK * HD:]
    return d_query, d_key, d_value, dw_key, dw_value
```

```python
import functools
import math

import jax
import jax.numpy as jnp
from jax import lax
from jax.experimental import pallas as pl
from jax.experimental.pallas import tpu as pltpu
from jax.sharding import PartitionSpec as P

HD = 128
WINDOW = 1024
TILE = 128

query_scale = 168.0 ** (-0.5)
masked_score = -1e30
EXP_SCALE = query_scale * math.log2(math.e)
F32 = jnp.float32
BF16 = jnp.bfloat16


def dot(a, b, contract):
    return lax.dot_general(a, b, ((contract[:1], contract[1:]), ((), ())), preferred_element_type=F32)


def kernel(n, fused, *refs):
    if fused:
        (seg_ref, q_ref, k_ref, v_ref, do_ref, x_hbm, dq_ref, dk_ref, dv_ref, dwk_ref, dwv_ref) = refs[:11]
        (kv, segs, segc, qs, dos, s_buf, dp_buf, pb, ds, dqt, out_g, in_g, kv_send, kv_recv, seg_send,
         seg_recv, g_send, g_recv, x_buf, xt, g_buf, one_out, one_in, two_out, two_in, three_out, three_in,
         one_send, one_recv, two_send, two_recv, three_send, three_recv, x_sem) = refs[11:]
    else:
        (seg_ref, q_ref, k_ref, v_ref, do_ref, dq_ref, dk_ref, dv_ref) = refs[:8]
        (kv, segs, segc, qs, dos, s_buf, dp_buf, pb, ds, dqt, out_g, in_g, kv_send, kv_recv, seg_send,
         seg_recv, g_send, g_recv) = refs[8:]
    me = lax.axis_index("ctx")
    rows = k_ref.shape[0]
    tiles = rows // TILE

    def remote(src, dst, send, recv, to):
        return pltpu.make_async_remote_copy(
            src_ref=src, dst_ref=dst, send_sem=send, recv_sem=recv,
            device_id={"ctx": to}, device_id_type=pl.DeviceIdType.MESH)

    if fused:
        x_copy = pltpu.make_async_copy(x_hbm, x_buf, x_sem)
        x_copy.start()
    barrier = pltpu.get_barrier_semaphore()
    near = [1, n - 1, 2, n - 2] + ([n // 2] if fused else [])
    for step in near:
        pl.semaphore_signal(barrier, inc=1, device_id={"ctx": lax.rem(me + step, n)},
                            device_id_type=pl.DeviceIdType.MESH)
    segs[0] = jnp.broadcast_to(seg_ref[...], (8, rows))
    kv[0, 0] = k_ref[...]
    kv[0, 1] = v_ref[...]
    pl.semaphore_wait(barrier, len(near))

    seg_copies, kv_copies = {}, {}
    for hop in (1, 2):
        to = lax.rem(me + hop, n)
        seg_copies[hop] = remote(segs.at[0], segs.at[hop], seg_send.at[hop - 1], seg_recv.at[hop - 1], to)
        for which in (0, 1):
            kv_copies[hop, which] = remote(kv.at[0, which], kv.at[hop, which], kv_send.at[hop - 1, which],
                                           kv_recv.at[hop - 1, which], to)
    for hop in (1, 2):
        seg_copies[hop].start()
    for which in (0, 1):
        for hop in (1, 2):
            kv_copies[hop, which].start()

    for head in (0, 1):
        qs[pl.ds(head * rows, rows), :] = q_ref[:, head * HD:(head + 1) * HD]
        dos[pl.ds(head * rows, rows), :] = do_ref[:, head * HD:(head + 1) * HD]
    seg_row = jnp.concatenate([seg_ref[...], seg_ref[...]], 1)

    def score_block(hop, top):
        column = segs[hop].T
        segc[...] = jnp.where(me >= hop, column, -1)

        def tile(t, top):
            at = pl.ds(pl.multiple_of(t * TILE, TILE), TILE)
            s = dot(kv[hop, 0, at, :], qs[...], (1, 1))
            allowed = segc[at, 0:1] == seg_row
            if hop != 1:
                k_pos = t * TILE + lax.broadcasted_iota(jnp.int32, (TILE, rows), 0)
                q_pos = lax.broadcasted_iota(jnp.int32, (TILE, rows), 1)
                inside = k_pos <= q_pos if hop == 0 else k_pos > q_pos
                allowed = allowed & jnp.concatenate([inside, inside], 1)
            s = jnp.where(allowed, s, masked_score)
            s_buf[hop, at, :] = s
            return jnp.maximum(top, jnp.max(s, 0, keepdims=True))

        return lax.fori_loop(0, tiles, tile, top)

    top = score_block(0, jnp.full((1, 2 * rows), masked_score, F32))
    if fused:
        x_copy.wait()
        wide = x_buf.shape[1]

        @pl.loop(0, wide // 128)
        def _(c):
            at = pl.ds(pl.multiple_of(c * 128, 128), 128)
            xt[at, :] = x_buf[:, at].T

    for hop in (1, 2):
        seg_copies[hop].wait()
        kv_copies[hop, 0].wait()
        top = score_block(hop, top)

    total = jnp.zeros((1, 2 * rows), F32)
    weighed = jnp.zeros((1, 2 * rows), F32)
    for hop in (0, 1, 2):
        if hop:
            kv_copies[hop, 1].wait()

        def tile(t, carry, hop=hop):
            total, weighed = carry
            at = pl.ds(pl.multiple_of(t * TILE, TILE), TILE)
            dp = dot(kv[hop, 1, at, :], dos[...], (1, 1))
            e = jnp.exp2((s_buf[hop, at, :] - top) * EXP_SCALE)
            s_buf[hop, at, :] = e
            dp_buf[hop, at, :] = dp
            return total + jnp.sum(e, 0, keepdims=True), weighed + jnp.sum(e * dp, 0, keepdims=True)

        total, weighed = lax.fori_loop(0, tiles, tile, (total, weighed))
    inverse = 1.0 / total
    delta = weighed * inverse

    g_copies = {}
    own = None
    for hop in (2, 1, 0):
        def tile(t, carry, hop=hop):
            at = pl.ds(pl.multiple_of(t * TILE, TILE), TILE)
            p = s_buf[hop, at, :] * inverse
            pb[at, :] = p.astype(BF16)
            ds[at, :] = (p * (dp_buf[hop, at, :] - delta)).astype(BF16)
            return carry

        lax.fori_loop(0, tiles, tile, 0)
        d_k = dot(ds[...], qs[...], (1, 0)) * query_scale
        d_v = dot(pb[...], dos[...], (1, 0))
        if hop:
            out_g[hop - 1, 0] = d_k.astype(BF16)
            out_g[hop - 1, 1] = d_v.astype(BF16)
            g_copies[hop] = remote(out_g.at[hop - 1], in_g.at[hop - 1], g_send.at[hop - 1], g_recv.at[hop - 1],
                                   lax.rem(me + n - hop, n))
            g_copies[hop].start()
        else:
            own = (d_k, d_v)
        dq_part = dot(kv[hop, 0].astype(F32).T.astype(BF16), ds[...], (1, 0))
        if hop == 2:
            dqt[...] = dq_part
        else:
            dqt[...] += dq_part
    for head in (0, 1):
        dq_ref[:, head * HD:(head + 1) * HD] = (
            dqt[:, head * rows:(head + 1) * rows].T * query_scale).astype(BF16)
    g_copies[2].wait()
    g_copies[1].wait()
    d_key = (own[0] + in_g[0, 0].astype(F32) + in_g[1, 0].astype(F32)).astype(BF16)
    d_value = (own[1] + in_g[0, 1].astype(F32) + in_g[1, 1].astype(F32)).astype(BF16)
    dk_ref[...] = d_key
    dv_ref[...] = d_value
    if not fused:
        return

    g_buf[:, :HD] = d_key
    g_buf[:, HD:] = d_value
    part = dwk_ref.shape[0]
    pair = me ^ 1
    side = me // 2

    def product(block):
        at = pl.ds(pl.multiple_of(block * part, 16), part)
        return dot(xt[at, :], g_buf[...], (1, 0))

    one, two, three = {}, {}, {}

    def for_pair(c):
        prod = product((side ^ c) * 2 + (pair & 1)).astype(BF16)
        one_out[c, 0] = prod[:, :HD]
        one_out[c, 1] = prod[:, HD:]
        one[c] = remote(one_out.at[c], one_in.at[c], one_send.at[c], one_recv.at[c], pair)
        one[c].start()

    def own_sum(c):
        prod = product((side ^ c) * 2 + (me & 1))
        one[c].wait()
        return prod[:, :HD] + one_in[c, 0].astype(F32), prod[:, HD:] + one_in[c, 1].astype(F32)

    over = (me ^ 2, me ^ 4)

    def send_two(half, slot, value):
        two_out[half, slot] = value.astype(BF16)
        two[half, slot] = remote(two_out.at[half, slot], two_in.at[half, slot], two_send.at[half, slot],
                                 two_recv.at[half, slot], over[half])
        two[half, slot].start()

    for_pair(3)
    for_pair(1)
    far = own_sum(3)
    send_two(0, 0, far[0])
    send_two(1, 0, far[1])
    for_pair(2)
    by_one = own_sum(1)
    send_two(0, 1, by_one[0])
    for_pair(0)
    by_two = own_sum(2)
    send_two(1, 1, by_two[1])
    mine = own_sum(0)

    def send_three(half, value):
        three_out[half] = value.astype(BF16)
        three[half] = remote(three_out.at[half], three_in.at[half], three_send.at[half], three_recv.at[half],
                             over[1 - half])
        three[half].start()

    two[0, 0].wait()
    send_three(0, by_two[0] + two_in[0, 0].astype(F32))
    two[1, 0].wait()
    send_three(1, by_one[1] + two_in[1, 0].astype(F32))
    two[0, 1].wait()
    two[1, 1].wait()
    for half, ref in ((0, dwk_ref), (1, dwv_ref)):
        ref[...] = mine[half] + two_in[half, 1].astype(F32)
    for half, ref in ((0, dwk_ref), (1, dwv_ref)):
        three[half].wait()
        ref[...] += three_in[half].astype(F32)


def body(n, tokens_in, query, key, value, d_out, seg_ids):
    rows, width = query.shape
    kv_width = key.shape[1]
    features = tokens_in.shape[1]
    part = features // n
    fused = n == 8 and part % 16 == 0
    dma = pltpu.SemaphoreType.DMA
    vmem = pltpu.VMEM
    out_shape = [
        jax.ShapeDtypeStruct((rows, width), BF16),
        jax.ShapeDtypeStruct((rows, kv_width), BF16),
        jax.ShapeDtypeStruct((rows, kv_width), BF16),
    ]
    scratch = [
        vmem((3, 2, rows, HD), BF16),
        vmem((3, 8, rows), jnp.int32),
        vmem((rows, 8), jnp.int32),
        vmem((2 * rows, HD), BF16),
        vmem((2 * rows, HD), BF16),
        vmem((3, rows, 2 * rows), F32),
        vmem((3, rows, 2 * rows), F32),
        vmem((rows, 2 * rows), BF16),
        vmem((rows, 2 * rows), BF16),
        vmem((HD, 2 * rows), F32),
        vmem((2, 2, rows, HD), BF16),
        vmem((2, 2, rows, HD), BF16),
        dma((2, 2)), dma((2, 2)), dma((2,)), dma((2,)), dma((2,)), dma((2,)),
    ]
    operands = [seg_ids.reshape(1, rows), query, key, value, d_out]
    in_specs = [pl.BlockSpec(memory_space=pltpu.VMEM)] * 5
    if fused:
        operands.append(tokens_in)
        in_specs = in_specs + [pl.BlockSpec(memory_space=pl.ANY)]
        out_shape += [jax.ShapeDtypeStruct((part, kv_width), F32)] * 2
        scratch += [
            vmem((rows, features), BF16),
            vmem((features, rows), BF16),
            vmem((rows, 2 * HD), BF16),
            vmem((4, 2, part, HD), BF16),
            vmem((4, 2, part, HD), BF16),
            vmem((2, 2, part, HD), BF16),
            vmem((2, 2, part, HD), BF16),
            vmem((2, part, HD), BF16),
            vmem((2, part, HD), BF16),
            dma((4,)), dma((4,)), dma((2, 2)), dma((2, 2)), dma((2,)), dma((2,)), dma,
        ]
    outs = pl.pallas_call(
        functools.partial(kernel, n, fused),
        out_shape=out_shape,
        in_specs=in_specs,
        out_specs=[pl.BlockSpec(memory_space=pltpu.VMEM)] * len(out_shape),
        scratch_shapes=scratch,
        compiler_params=pltpu.CompilerParams(
            collective_id=0, has_side_effects=True, vmem_limit_bytes=56 * 1024 * 1024),
    )(*operands)
    if fused:
        return tuple(outs)
    d_query, d_key, d_value = outs
    grads_both = jnp.concatenate([d_key, d_value], 1)
    summed = lax.psum_scatter(
        dot(tokens_in, grads_both, (0, 0)).astype(BF16), "ctx", scatter_dimension=0, tiled=True
    ).astype(F32)
    return (d_query, d_key, d_value, summed[:, :kv_width], summed[:, kv_width:])


def solution(mesh):
    n = mesh.shape["ctx"]
    in_specs = (P("ctx", None),) + (P("ctx", "fsdp"),) * 4 + (P("ctx"),)
    return jax.shard_map(functools.partial(body, n), mesh=mesh, in_specs=in_specs,
                         out_specs=(P("ctx", "fsdp"),) * 5, check_vma=False)
```

```python
import functools
import math

import jax
import jax.numpy as jnp
from jax import lax
from jax.experimental import pallas as pl
from jax.experimental.pallas import tpu as pltpu
from jax.sharding import PartitionSpec as P

HD = 128
WINDOW = 1024
TILE = 128

query_scale = 168.0 ** (-0.5)
masked_score = -1e30
EXP_SCALE = query_scale * math.log2(math.e)
F32 = jnp.float32
BF16 = jnp.bfloat16


def dot(a, b, contract):
    return lax.dot_general(a, b, ((contract[:1], contract[1:]), ((), ())), preferred_element_type=F32)


def kernel(n, fused, *refs):
    if fused:
        (seg_ref, q_ref, k_ref, v_ref, do_ref, x_hbm, dq_ref, dk_ref, dv_ref, dwk_ref, dwv_ref) = refs[:11]
        (kv, segs, segc, qs, dos, s_buf, dp_buf, pb, ds, dqt, out_g, in_g, kv_send, kv_recv, seg_send,
         seg_recv, g_send, g_recv, x_buf, xt, g_buf, one_out, one_in, two_out, two_in, three_out, three_in,
         one_send, one_recv, two_send, two_recv, three_send, three_recv, x_sem) = refs[11:]
    else:
        (seg_ref, q_ref, k_ref, v_ref, do_ref, dq_ref, dk_ref, dv_ref) = refs[:8]
        (kv, segs, segc, qs, dos, s_buf, dp_buf, pb, ds, dqt, out_g, in_g, kv_send, kv_recv, seg_send,
         seg_recv, g_send, g_recv) = refs[8:]
    me = lax.axis_index("ctx")
    rows = k_ref.shape[0]
    tiles = rows // TILE

    def remote(src, dst, send, recv, to):
        return pltpu.make_async_remote_copy(
            src_ref=src, dst_ref=dst, send_sem=send, recv_sem=recv,
            device_id={"ctx": to}, device_id_type=pl.DeviceIdType.MESH)

    if fused:
        x_copy = pltpu.make_async_copy(x_hbm, x_buf, x_sem)
        x_copy.start()
    barrier = pltpu.get_barrier_semaphore()
    near = [1, n - 1, 2, n - 2] + ([n // 2] if fused else [])
    for step in near:
        pl.semaphore_signal(barrier, inc=1, device_id={"ctx": lax.rem(me + step, n)},
                            device_id_type=pl.DeviceIdType.MESH)
    segs[0] = jnp.broadcast_to(seg_ref[...], (8, rows))
    kv[0, 0] = k_ref[...]
    kv[0, 1] = v_ref[...]
    pl.semaphore_wait(barrier, len(near))

    seg_copies, kv_copies = {}, {}
    for hop in (1, 2):
        to = lax.rem(me + hop, n)
        seg_copies[hop] = remote(segs.at[0], segs.at[hop], seg_send.at[hop - 1], seg_recv.at[hop - 1], to)
        for which in (0, 1):
            kv_copies[hop, which] = remote(kv.at[0, which], kv.at[hop, which], kv_send.at[hop - 1, which],
                                           kv_recv.at[hop - 1, which], to)
    for hop in (1, 2):
        seg_copies[hop].start()
    for which in (0, 1):
        for hop in (1, 2):
            kv_copies[hop, which].start()

    for head in (0, 1):
        qs[pl.ds(head * rows, rows), :] = q_ref[:, head * HD:(head + 1) * HD]
        dos[pl.ds(head * rows, rows), :] = do_ref[:, head * HD:(head + 1) * HD]
    seg_row = jnp.concatenate([seg_ref[...], seg_ref[...]], 1)

    def by_tiles(step, carry):
        def tile(t, carry):
            return step(t, pl.ds(pl.multiple_of(t * TILE, TILE), TILE), carry)

        return lax.fori_loop(0, tiles, tile, carry)

    def score_block(hop, top):
        segc[...] = jnp.where(me >= hop, segs[hop].T, -1)

        def step(t, at, top):
            s = dot(kv[hop, 0, at, :], qs[...], (1, 1))
            allowed = segc[at, 0:1] == seg_row
            if hop != 1:
                k_pos = t * TILE + lax.broadcasted_iota(jnp.int32, (TILE, rows), 0)
                q_pos = lax.broadcasted_iota(jnp.int32, (TILE, rows), 1)
                inside = k_pos <= q_pos if hop == 0 else k_pos > q_pos
                allowed = allowed & jnp.concatenate([inside, inside], 1)
            s = jnp.where(allowed, s, masked_score)
            s_buf[hop, at, :] = s
            return jnp.maximum(top, jnp.max(s, 0, keepdims=True))

        return by_tiles(step, top)

    def turn_tokens(first, last):
        @pl.loop(first, last)
        def _(c):
            at = pl.ds(pl.multiple_of(c * 128, 128), 128)
            xt[at, :] = x_buf[:, at].T

    top = score_block(0, jnp.full((1, 2 * rows), masked_score, F32))
    if fused:
        blocks = x_buf.shape[1] // 128
        early = blocks // 2
        x_copy.wait()
        turn_tokens(0, early)
    for hop in (1, 2):
        seg_copies[hop].wait()
        kv_copies[hop, 0].wait()
        top = score_block(hop, top)

    total = jnp.zeros((1, 2 * rows), F32)
    for hop in (0, 1, 2):
        def step(t, at, total, hop=hop):
            e = jnp.exp2((s_buf[hop, at, :] - top) * EXP_SCALE)
            s_buf[hop, at, :] = e
            return total + jnp.sum(e, 0, keepdims=True)

        total = by_tiles(step, total)
    inverse = 1.0 / total

    g_copies = {}
    own = {}

    def give(hop, which, value):
        if hop == 0:
            own[which] = value
            return
        out_g[hop - 1, which] = value.astype(BF16)
        g_copies[hop, which] = remote(out_g.at[hop - 1, which], in_g.at[hop - 1, which], g_send.at[hop - 1, which],
                                      g_recv.at[hop - 1, which], lax.rem(me + n - hop, n))
        g_copies[hop, which].start()

    for hop in (2, 1, 0):
        def step(t, at, carry, hop=hop):
            p = s_buf[hop, at, :] * inverse
            s_buf[hop, at, :] = p
            pb[at, :] = p.astype(BF16)
            return carry

        by_tiles(step, 0)
        give(hop, 1, dot(pb[...], dos[...], (1, 0)))

    delta = jnp.zeros((1, 2 * rows), F32)
    for hop in (0, 1, 2):
        if hop:
            kv_copies[hop, 1].wait()

        def step(t, at, delta, hop=hop):
            dp = dot(kv[hop, 1, at, :], dos[...], (1, 1))
            dp_buf[hop, at, :] = dp
            return delta + jnp.sum(s_buf[hop, at, :] * dp, 0, keepdims=True)

        delta = by_tiles(step, delta)

    for hop in (2, 1, 0):
        def step(t, at, carry, hop=hop):
            ds[hop, at, :] = (s_buf[hop, at, :] * (dp_buf[hop, at, :] - delta)).astype(BF16)
            return carry

        by_tiles(step, 0)
        give(hop, 0, dot(ds[hop], qs[...], (1, 0)) * query_scale)
    for hop in (2, 1, 0):
        dq_part = dot(kv[hop, 0].astype(F32).T.astype(BF16), ds[hop], (1, 0))
        if hop == 2:
            dqt[...] = dq_part
        else:
            dqt[...] += dq_part
    for head in (0, 1):
        dq_ref[:, head * HD:(head + 1) * HD] = (
            dqt[:, head * rows:(head + 1) * rows].T * query_scale).astype(BF16)
    if fused:
        turn_tokens(early, blocks)
    for which in (1, 0):
        for hop in (2, 1):
            g_copies[hop, which].wait()
    d_key = (own[0] + in_g[0, 0].astype(F32) + in_g[1, 0].astype(F32)).astype(BF16)
    d_value = (own[1] + in_g[0, 1].astype(F32) + in_g[1, 1].astype(F32)).astype(BF16)
    dk_ref[...] = d_key
    dv_ref[...] = d_value
    if not fused:
        return

    g_buf[:, :HD] = d_key
    g_buf[:, HD:] = d_value
    part = dwk_ref.shape[0]
    pair = me ^ 1
    side = me // 2

    def product(block):
        at = pl.ds(pl.multiple_of(block * part, 16), part)
        return dot(xt[at, :], g_buf[...], (1, 0))

    one, two, three = {}, {}, {}

    def for_pair(c):
        prod = product((side ^ c) * 2 + (pair & 1)).astype(BF16)
        one_out[c, 0] = prod[:, :HD]
        one_out[c, 1] = prod[:, HD:]
        one[c] = remote(one_out.at[c], one_in.at[c], one_send.at[c], one_recv.at[c], pair)
        one[c].start()

    def own_sum(c):
        prod = product((side ^ c) * 2 + (me & 1))
        one[c].wait()
        return prod[:, :HD] + one_in[c, 0].astype(F32), prod[:, HD:] + one_in[c, 1].astype(F32)

    over = (me ^ 2, me ^ 4)

    def send_two(half, slot, value):
        two_out[half, slot] = value.astype(BF16)
        two[half, slot] = remote(two_out.at[half, slot], two_in.at[half, slot], two_send.at[half, slot],
                                 two_recv.at[half, slot], over[half])
        two[half, slot].start()

    for_pair(3)
    for_pair(1)
    far = own_sum(3)
    send_two(0, 0, far[0])
    send_two(1, 0, far[1])
    for_pair(2)
    by_one = own_sum(1)
    send_two(0, 1, by_one[0])
    for_pair(0)
    by_two = own_sum(2)
    send_two(1, 1, by_two[1])
    mine = own_sum(0)

    def send_three(half, value):
        three_out[half] = value.astype(BF16)
        three[half] = remote(three_out.at[half], three_in.at[half], three_send.at[half], three_recv.at[half],
                             over[1 - half])
        three[half].start()

    two[0, 0].wait()
    send_three(0, by_two[0] + two_in[0, 0].astype(F32))
    two[1, 0].wait()
    send_three(1, by_one[1] + two_in[1, 0].astype(F32))
    two[0, 1].wait()
    two[1, 1].wait()
    for half, ref in ((0, dwk_ref), (1, dwv_ref)):
        ref[...] = mine[half] + two_in[half, 1].astype(F32)
    for half, ref in ((0, dwk_ref), (1, dwv_ref)):
        three[half].wait()
        ref[...] += three_in[half].astype(F32)


def hand_on(*refs):
    count = len(refs) // 2
    for i in range(count):
        refs[count + i][...] = refs[i][...]


def body(n, tokens_in, query, key, value, d_out, seg_ids):
    rows, width = query.shape
    kv_width = key.shape[1]
    features = tokens_in.shape[1]
    part = features // n
    fused = n == 8 and part % 16 == 0
    dma = pltpu.SemaphoreType.DMA
    vmem = pltpu.VMEM
    out_shape = [
        jax.ShapeDtypeStruct((rows, width), BF16),
        jax.ShapeDtypeStruct((rows, kv_width), BF16),
        jax.ShapeDtypeStruct((rows, kv_width), BF16),
    ]
    scratch = [
        vmem((3, 2, rows, HD), BF16),
        vmem((3, 8, rows), jnp.int32),
        vmem((rows, 8), jnp.int32),
        vmem((2 * rows, HD), BF16),
        vmem((2 * rows, HD), BF16),
        vmem((3, rows, 2 * rows), F32),
        vmem((3, rows, 2 * rows), F32),
        vmem((rows, 2 * rows), BF16),
        vmem((3, rows, 2 * rows), BF16),
        vmem((HD, 2 * rows), F32),
        vmem((2, 2, rows, HD), BF16),
        vmem((2, 2, rows, HD), BF16),
        dma((2, 2)), dma((2, 2)), dma((2,)), dma((2,)), dma((2, 2)), dma((2, 2)),
    ]
    operands = [seg_ids.reshape(1, rows), query, key, value, d_out]
    in_specs = [pl.BlockSpec(memory_space=pltpu.VMEM)] * 5
    if fused:
        operands.append(tokens_in)
        in_specs = in_specs + [pl.BlockSpec(memory_space=pl.ANY)]
        out_shape += [jax.ShapeDtypeStruct((part, kv_width), F32)] * 2
        scratch += [
            vmem((rows, features), BF16),
            vmem((features, rows), BF16),
            vmem((rows, 2 * HD), BF16),
            vmem((4, 2, part, HD), BF16),
            vmem((4, 2, part, HD), BF16),
            vmem((2, 2, part, HD), BF16),
            vmem((2, 2, part, HD), BF16),
            vmem((2, part, HD), BF16),
            vmem((2, part, HD), BF16),
            dma((4,)), dma((4,)), dma((2, 2)), dma((2, 2)), dma((2,)), dma((2,)), dma,
        ]
    outs = pl.pallas_call(
        functools.partial(kernel, n, fused),
        out_shape=out_shape,
        in_specs=in_specs,
        out_specs=[pl.BlockSpec(memory_space=pltpu.VMEM)] * len(out_shape),
        scratch_shapes=scratch,
        compiler_params=pltpu.CompilerParams(
            collective_id=0, has_side_effects=True, vmem_limit_bytes=56 * 1024 * 1024),
    )(*operands)
    if fused:
        whole = pl.BlockSpec(memory_space=pltpu.VMEM)
        return tuple(pl.pallas_call(
            hand_on, out_shape=out_shape, in_specs=[whole] * 5, out_specs=[whole] * 5,
        )(*outs))
    d_query, d_key, d_value = outs
    grads_both = jnp.concatenate([d_key, d_value], 1)
    summed = lax.psum_scatter(
        dot(tokens_in, grads_both, (0, 0)).astype(BF16), "ctx", scatter_dimension=0, tiled=True
    ).astype(F32)
    return (d_query, d_key, d_value, summed[:, :kv_width], summed[:, kv_width:])


def solution(mesh):
    n = mesh.shape["ctx"]
    in_specs = (P("ctx", None),) + (P("ctx", "fsdp"),) * 4 + (P("ctx"),)
    return jax.shard_map(functools.partial(body, n), mesh=mesh, in_specs=in_specs,
                         out_specs=(P("ctx", "fsdp"),) * 5, check_vma=False)
```

```python
import functools
import math

import jax
import jax.numpy as jnp
from jax import lax
from jax.experimental import pallas as pl
from jax.experimental.pallas import tpu as pltpu
from jax.sharding import PartitionSpec as P

HD = 128
WINDOW = 1024
TILE = 128

query_scale = 168.0 ** (-0.5)
masked_score = -1e30
EXP_SCALE = query_scale * math.log2(math.e)
F32 = jnp.float32
BF16 = jnp.bfloat16


def dot(a, b, contract):
    return lax.dot_general(a, b, ((contract[:1], contract[1:]), ((), ())), preferred_element_type=F32)


def kernel(n, fused, *refs):
    if fused:
        (seg_ref, q_ref, k_ref, v_ref, do_ref, x_hbm, dq_ref, dk_ref, dv_ref, dwk_ref, dwv_ref) = refs[:11]
        (kv, segs, segc, qs, dos, s_buf, dp_buf, pb, ds, dqt, out_g, in_g, kv_send, kv_recv, seg_send,
         seg_recv, g_send, g_recv, x_buf, xt, g_buf, one_out, one_in, two_out, two_in, three_out, three_in,
         one_send, one_recv, two_send, two_recv, three_send, three_recv, x_sem) = refs[11:]
    else:
        (seg_ref, q_ref, k_ref, v_ref, do_ref, dq_ref, dk_ref, dv_ref) = refs[:8]
        (kv, segs, segc, qs, dos, s_buf, dp_buf, pb, ds, dqt, out_g, in_g, kv_send, kv_recv, seg_send,
         seg_recv, g_send, g_recv) = refs[8:]
    me = lax.axis_index("ctx")
    rows = k_ref.shape[0]
    tiles = rows // TILE

    def remote(src, dst, send, recv, to):
        return pltpu.make_async_remote_copy(
            src_ref=src, dst_ref=dst, send_sem=send, recv_sem=recv,
            device_id={"ctx": to}, device_id_type=pl.DeviceIdType.MESH)

    if fused:
        x_copy = pltpu.make_async_copy(x_hbm, x_buf, x_sem)
        x_copy.start()
    barrier = pltpu.get_barrier_semaphore()
    near = [1, n - 1, 2, n - 2] + ([n // 2] if fused else [])
    for step in near:
        pl.semaphore_signal(barrier, inc=1, device_id={"ctx": lax.rem(me + step, n)},
                            device_id_type=pl.DeviceIdType.MESH)
    segs[0] = jnp.broadcast_to(seg_ref[...], (8, rows))
    kv[0, 0] = k_ref[...]
    kv[0, 1] = v_ref[...]
    pl.semaphore_wait(barrier, len(near))

    seg_copies, kv_copies = {}, {}
    for hop in (1, 2):
        to = lax.rem(me + hop, n)
        seg_copies[hop] = remote(segs.at[0], segs.at[hop], seg_send.at[hop - 1], seg_recv.at[hop - 1], to)
        for which in (0, 1):
            kv_copies[hop, which] = remote(kv.at[0, which], kv.at[hop, which], kv_send.at[hop - 1, which],
                                           kv_recv.at[hop - 1, which], to)
    for hop in (1, 2):
        seg_copies[hop].start()
    for which in (0, 1):
        for hop in (1, 2):
            kv_copies[hop, which].start()

    for head in (0, 1):
        qs[pl.ds(head * rows, rows), :] = q_ref[:, head * HD:(head + 1) * HD]
        dos[pl.ds(head * rows, rows), :] = do_ref[:, head * HD:(head + 1) * HD]
    seg_row = jnp.concatenate([seg_ref[...], seg_ref[...]], 1)

    def by_tiles(step, carry):
        def tile(t, carry):
            return step(t, pl.ds(pl.multiple_of(t * TILE, TILE), TILE), carry)

        return lax.fori_loop(0, tiles, tile, carry, unroll=2)

    def score_block(hop, top):
        segc[...] = jnp.where(me >= hop, segs[hop].T, -1)

        def step(t, at, top):
            s = dot(kv[hop, 0, at, :], qs[...], (1, 1))
            allowed = segc[at, 0:1] == seg_row
            if hop != 1:
                k_pos = t * TILE + lax.broadcasted_iota(jnp.int32, (TILE, rows), 0)
                q_pos = lax.broadcasted_iota(jnp.int32, (TILE, rows), 1)
                inside = k_pos <= q_pos if hop == 0 else k_pos > q_pos
                allowed = allowed & jnp.concatenate([inside, inside], 1)
            s = jnp.where(allowed, s, masked_score)
            s_buf[hop, at, :] = s
            return jnp.maximum(top, jnp.max(s, 0, keepdims=True))

        return by_tiles(step, top)

    def turn_tokens(first, last):
        @pl.loop(first, last)
        def _(c):
            at = pl.ds(pl.multiple_of(c * 128, 128), 128)
            xt[at, :] = x_buf[:, at].T

    top = score_block(0, jnp.full((1, 2 * rows), masked_score, F32))
    if fused:
        blocks = x_buf.shape[1] // 128
        early = blocks // 2
        x_copy.wait()
        turn_tokens(0, early)
    for hop in (1, 2):
        seg_copies[hop].wait()
        kv_copies[hop, 0].wait()
        top = score_block(hop, top)

    total = jnp.zeros((1, 2 * rows), F32)
    for hop in (0, 1, 2):
        def step(t, at, total, hop=hop):
            e = jnp.exp2((s_buf[hop, at, :] - top) * EXP_SCALE)
            s_buf[hop, at, :] = e
            return total + jnp.sum(e, 0, keepdims=True)

        total = by_tiles(step, total)
    inverse = 1.0 / total

    g_copies = {}
    own = {}

    def give(hop, which, value):
        if hop == 0:
            own[which] = value
            return
        out_g[hop - 1, which] = value.astype(BF16)
        g_copies[hop, which] = remote(out_g.at[hop - 1, which], in_g.at[hop - 1, which], g_send.at[hop - 1, which],
                                      g_recv.at[hop - 1, which], lax.rem(me + n - hop, n))
        g_copies[hop, which].start()

    for hop in (2, 1, 0):
        def step(t, at, carry, hop=hop):
            pb[at, :] = (s_buf[hop, at, :] * inverse).astype(BF16)
            return carry

        by_tiles(step, 0)
        give(hop, 1, dot(pb[...], dos[...], (1, 0)))

    delta = jnp.zeros((1, 2 * rows), F32)
    for hop in (0, 1, 2):
        if hop:
            kv_copies[hop, 1].wait()

        def step(t, at, delta, hop=hop):
            dp = dot(kv[hop, 1, at, :], dos[...], (1, 1))
            dp_buf[hop, at, :] = dp
            return delta + jnp.sum(s_buf[hop, at, :] * dp, 0, keepdims=True)

        delta = by_tiles(step, delta)
    delta = delta * inverse

    for hop in (2, 1, 0):
        def step(t, at, carry, hop=hop):
            ds[hop, at, :] = (s_buf[hop, at, :] * inverse * (dp_buf[hop, at, :] - delta)).astype(BF16)
            return carry

        by_tiles(step, 0)
        give(hop, 0, dot(ds[hop], qs[...], (1, 0)) * query_scale)
    for hop in (2, 1, 0):
        dq_part = dot(kv[hop, 0].astype(F32).T.astype(BF16), ds[hop], (1, 0))
        if hop == 2:
            dqt[...] = dq_part
        else:
            dqt[...] += dq_part
    for head in (0, 1):
        dq_ref[:, head * HD:(head + 1) * HD] = (
            dqt[:, head * rows:(head + 1) * rows].T * query_scale).astype(BF16)
    if fused:
        turn_tokens(early, blocks)
    for which in (1, 0):
        for hop in (2, 1):
            g_copies[hop, which].wait()
    d_key = (own[0] + in_g[0, 0].astype(F32) + in_g[1, 0].astype(F32)).astype(BF16)
    d_value = (own[1] + in_g[0, 1].astype(F32) + in_g[1, 1].astype(F32)).astype(BF16)
    dk_ref[...] = d_key
    dv_ref[...] = d_value
    if not fused:
        return

    g_buf[:, :HD] = d_key
    g_buf[:, HD:] = d_value
    part = dwk_ref.shape[0]
    pair = me ^ 1
    side = me // 2

    def product(block):
        at = pl.ds(pl.multiple_of(block * part, 16), part)
        return dot(xt[at, :], g_buf[...], (1, 0))

    one, two, three = {}, {}, {}

    def for_pair(c):
        prod = product((side ^ c) * 2 + (pair & 1)).astype(BF16)
        one_out[c, 0] = prod[:, :HD]
        one_out[c, 1] = prod[:, HD:]
        one[c] = remote(one_out.at[c], one_in.at[c], one_send.at[c], one_recv.at[c], pair)
        one[c].start()

    def own_sum(c):
        prod = product((side ^ c) * 2 + (me & 1))
        one[c].wait()
        return prod[:, :HD] + one_in[c, 0].astype(F32), prod[:, HD:] + one_in[c, 1].astype(F32)

    over = (me ^ 2, me ^ 4)

    def send_two(half, slot, value):
        two_out[half, slot] = value.astype(BF16)
        two[half, slot] = remote(two_out.at[half, slot], two_in.at[half, slot], two_send.at[half, slot],
                                 two_recv.at[half, slot], over[half])
        two[half, slot].start()

    for_pair(3)
    for_pair(1)
    far = own_sum(3)
    send_two(0, 0, far[0])
    send_two(1, 0, far[1])
    for_pair(2)
    by_one = own_sum(1)
    send_two(0, 1, by_one[0])
    for_pair(0)
    by_two = own_sum(2)
    send_two(1, 1, by_two[1])
    mine = own_sum(0)

    def send_three(half, value):
        three_out[half] = value.astype(BF16)
        three[half] = remote(three_out.at[half], three_in.at[half], three_send.at[half], three_recv.at[half],
                             over[1 - half])
        three[half].start()

    two[0, 0].wait()
    send_three(0, by_two[0] + two_in[0, 0].astype(F32))
    two[1, 0].wait()
    send_three(1, by_one[1] + two_in[1, 0].astype(F32))
    two[0, 1].wait()
    two[1, 1].wait()
    for half, ref in ((0, dwk_ref), (1, dwv_ref)):
        ref[...] = mine[half] + two_in[half, 1].astype(F32)
    for half, ref in ((0, dwk_ref), (1, dwv_ref)):
        three[half].wait()
        ref[...] += three_in[half].astype(F32)


def hand_on(*refs):
    count = len(refs) // 2
    for i in range(count):
        refs[count + i][...] = refs[i][...]


def body(n, tokens_in, query, key, value, d_out, seg_ids):
    rows, width = query.shape
    kv_width = key.shape[1]
    features = tokens_in.shape[1]
    part = features // n
    fused = n == 8 and part % 16 == 0
    dma = pltpu.SemaphoreType.DMA
    vmem = pltpu.VMEM
    out_shape = [
        jax.ShapeDtypeStruct((rows, width), BF16),
        jax.ShapeDtypeStruct((rows, kv_width), BF16),
        jax.ShapeDtypeStruct((rows, kv_width), BF16),
    ]
    scratch = [
        vmem((3, 2, rows, HD), BF16),
        vmem((3, 8, rows), jnp.int32),
        vmem((rows, 8), jnp.int32),
        vmem((2 * rows, HD), BF16),
        vmem((2 * rows, HD), BF16),
        vmem((3, rows, 2 * rows), F32),
        vmem((3, rows, 2 * rows), F32),
        vmem((rows, 2 * rows), BF16),
        vmem((3, rows, 2 * rows), BF16),
        vmem((HD, 2 * rows), F32),
        vmem((2, 2, rows, HD), BF16),
        vmem((2, 2, rows, HD), BF16),
        dma((2, 2)), dma((2, 2)), dma((2,)), dma((2,)), dma((2, 2)), dma((2, 2)),
    ]
    operands = [seg_ids.reshape(1, rows), query, key, value, d_out]
    in_specs = [pl.BlockSpec(memory_space=pltpu.VMEM)] * 5
    if fused:
        operands.append(tokens_in)
        in_specs = in_specs + [pl.BlockSpec(memory_space=pl.ANY)]
        out_shape += [jax.ShapeDtypeStruct((part, kv_width), F32)] * 2
        scratch += [
            vmem((rows, features), BF16),
            vmem((features, rows), BF16),
            vmem((rows, 2 * HD), BF16),
            vmem((4, 2, part, HD), BF16),
            vmem((4, 2, part, HD), BF16),
            vmem((2, 2, part, HD), BF16),
            vmem((2, 2, part, HD), BF16),
            vmem((2, part, HD), BF16),
            vmem((2, part, HD), BF16),
            dma((4,)), dma((4,)), dma((2, 2)), dma((2, 2)), dma((2,)), dma((2,)), dma,
        ]
    outs = pl.pallas_call(
        functools.partial(kernel, n, fused),
        out_shape=out_shape,
        in_specs=in_specs,
        out_specs=[pl.BlockSpec(memory_space=pltpu.VMEM)] * len(out_shape),
        scratch_shapes=scratch,
        compiler_params=pltpu.CompilerParams(
            collective_id=0, has_side_effects=True, vmem_limit_bytes=56 * 1024 * 1024),
    )(*operands)
    if fused:
        whole = pl.BlockSpec(memory_space=pltpu.VMEM)
        return tuple(pl.pallas_call(
            hand_on, out_shape=out_shape, in_specs=[whole] * 5, out_specs=[whole] * 5,
        )(*outs))
    d_query, d_key, d_value = outs
    grads_both = jnp.concatenate([d_key, d_value], 1)
    summed = lax.psum_scatter(
        dot(tokens_in, grads_both, (0, 0)).astype(BF16), "ctx", scatter_dimension=0, tiled=True
    ).astype(F32)
    return (d_query, d_key, d_value, summed[:, :kv_width], summed[:, kv_width:])


def solution(mesh):
    n = mesh.shape["ctx"]
    in_specs = (P("ctx", None),) + (P("ctx", "fsdp"),) * 4 + (P("ctx"),)
    return jax.shard_map(functools.partial(body, n), mesh=mesh, in_specs=in_specs,
                         out_specs=(P("ctx", "fsdp"),) * 5, check_vma=False)
```
